32 devices in a mesh: groups: 2 (over x), seq: 16 (over z, y, core).
Axes of the slice: x: 2, y: 2, z: 4, core: 2. Of those that a mesh axis runs over, the one named last changes fastest.
Arguments:
- clip_tokens: bfloat16 [32, 128, 512], P(('groups', 'seq')), parts along dimension 0, may hold values from -6 to 6
- spatial_qkv: bfloat16 [512, 1536], replicated, may hold values from -4.6403883 to 4.6403883
- spatial_out: bfloat16 [512, 512], replicated, may hold values from -0.5 to 0.5
- temporal_qkv: bfloat16 [512, 1536], replicated, may hold values from -4.6403883 to 4.6403883
- temporal_out: bfloat16 [512, 512], replicated, may hold values from -0.5 to 0.5
- mlp_up: bfloat16 [512, 2048], replicated, may hold values from -0.25 to 0.25
- mlp_down: bfloat16 [2048, 512], replicated, may hold values from -0.25 to 0.25
Outputs:
- layer_out: bfloat16 [32, 128, 512], P(('groups', 'seq')), parts along dimension 0
The draws below stay inside these ranges and needn't reach their ends.
There are 2 independent parts, one for each index of `groups`. The reference program is written for one: setup_inputs(seed, part) draws one part's arguments, and reference() takes and returns one part's arrays. A program takes and returns all parts, laid end to end along the dimension named above; an argument that names none is the same for every part. Nothing has to cross between parts.
All inputs are finite; a program needn't handle non-finite values.
Results may differ from the reference program's by a relative error of at most 0.013.
Values may be sent and summed in bfloat16 or wider, within the bound.
No kernel may reach another device: no remote copies, remote signals or barrier semaphores. Data moves between devices by JAX's collectives and lax.ppermute only.
A program may use at most 128 MiB of HBM per device.

```python
import jax
import jax.numpy as jnp
from jax import lax

D = 512
HEADS = 8
HEAD_DIM = 64
FF = 2048
PATCH_DEV = 8
FRAMES = 16
PATCHES = 128


def projection_draw(key):
    scale = D ** (-0.5)
    matrix_draw = jnp.clip(jax.random.normal(key, (D, 3 * D), jnp.float32), -5.0, 5.0) * scale
    return matrix_draw.astype(jnp.bfloat16)


def draw_spatial_qkv(key, part):
    return projection_draw(jax.random.fold_in(key, 101))


def draw_temporal_qkv(key, part):
    return projection_draw(jax.random.fold_in(key, 202))


def shard_levels(rng, dims, shards, smallest, top_value):
    def one(axis_at, shards_of):
        steps = jax.random.uniform(jax.random.fold_in(jax.random.fold_in(rng, 6), axis_at), (shards_of,), jnp.float32, smallest / len(shards), top_value / len(shards))
        return jnp.repeat(jnp.exp(steps), dims[axis_at] // shards_of).reshape((-1,) + (1,) * (len(dims) - axis_at - 1))

    gain = one(*shards[0])
    for cut in shards[1:]:
        gain = gain * one(*cut)
    return gain


def gaussian(key, extent, deviation, reach, split=(), held_as=jnp.bfloat16):
    drawn = jax.random.normal(key, extent, jnp.float32) * deviation
    if len(split) > 0:
        drawn = shard_levels(key, extent, split, -0.22, 0.18) * drawn
    return jnp.clip(drawn, min=-reach, max=reach).astype(held_as)


def setup_inputs(seed: int = 0, part: int = 0) -> dict:
    streams_of = jax.random.split(jax.random.key(seed), 8)
    own_keys = jax.random.split(jax.random.fold_in(streams_of[7], part), 8)
    clip_tokens = gaussian(own_keys[0], (FRAMES, PATCHES, D), 1.0, 6.0, ((0, 16),))
    spatial_qkv = draw_spatial_qkv(jax.random.fold_in(streams_of[7], 71), part)
    spatial_out = gaussian(streams_of[2], (D, D), (D // 4) ** -0.5, 0.5)
    temporal_qkv = draw_temporal_qkv(jax.random.fold_in(streams_of[7], 71), part)
    temporal_out = gaussian(streams_of[4], (D, D), (D // 4) ** -0.5, 0.5)
    mlp_up = gaussian(streams_of[5], (D, FF), D ** -0.5, 0.25)
    mlp_down = gaussian(streams_of[6], (FF, D), (FF // 4) ** -0.5, 0.25)
    return {"clip_tokens": clip_tokens, "spatial_qkv": spatial_qkv, "spatial_out": spatial_out, "temporal_qkv": temporal_qkv, "temporal_out": temporal_out, "mlp_up": mlp_up, "mlp_down": mlp_down}


def norm_rows(values):
    center = values - lax.optimization_barrier(jnp.mean(values, axis=-1, keepdims=True))
    spread = lax.optimization_barrier(jnp.mean(center * center, axis=-1, keepdims=True))
    return (center * lax.rsqrt(spread + 1e-05)).astype(jnp.bfloat16)

def softmax_rows(scores):
    row_max = lax.optimization_barrier(jnp.max(scores, axis=-1, keepdims=True))
    raised = jnp.exp(scores - row_max)
    return (raised / lax.optimization_barrier(jnp.sum(raised, axis=-1, keepdims=True))).astype(jnp.bfloat16)

def spatial_frame(frame_rows, w_qkv, w_out):
    packed = jnp.dot(norm_rows(frame_rows.astype(jnp.float32)), w_qkv, preferred_element_type=jnp.float32)
    packed = packed.astype(jnp.bfloat16).reshape(PATCHES, 3, HEADS, HEAD_DIM).astype(jnp.float32)
    scores = jnp.einsum('qhd,khd->hqk', packed[:, 0], packed[:, 1]) * HEAD_DIM ** (-0.5)
    weights = softmax_rows(scores).astype(jnp.float32)
    attended = jnp.einsum('hqk,khd->qhd', weights, packed[:, 2]).astype(jnp.bfloat16).reshape(PATCHES, D)
    merged = frame_rows.astype(jnp.float32) + jnp.dot(attended, w_out, preferred_element_type=jnp.float32)
    return merged.astype(jnp.bfloat16)

def temporal_block(tokens, w_qkv, w_out):
    frames, count_rows, model_width = tokens.shape
    flat_rows = tokens.reshape(frames * count_rows, model_width)
    packed = jnp.dot(norm_rows(flat_rows.astype(jnp.float32)), w_qkv, preferred_element_type=jnp.float32)
    packed = packed.astype(jnp.bfloat16).reshape(frames, count_rows, 3, HEADS, HEAD_DIM).astype(jnp.float32)
    scores = jnp.einsum('fkhd,gkhd->khfg', packed[:, :, 0], packed[:, :, 1]) * HEAD_DIM ** (-0.5)
    weights = softmax_rows(scores).astype(jnp.float32)
    attended = jnp.einsum('khfg,gkhd->fkhd', weights, packed[:, :, 2]).astype(jnp.bfloat16)
    attended = attended.reshape(frames * count_rows, model_width)
    merged = flat_rows.astype(jnp.float32) + jnp.dot(attended, w_out, preferred_element_type=jnp.float32)
    return merged.astype(jnp.bfloat16)

def feed_forward(tokens, w_up, w_down):
    raised = jnp.dot(norm_rows(tokens.astype(jnp.float32)), w_up, preferred_element_type=jnp.float32)
    hidden = jax.nn.gelu(raised, approximate=True).astype(jnp.bfloat16)
    merged = tokens.astype(jnp.float32) + jnp.dot(hidden, w_down, preferred_element_type=jnp.float32)
    return merged.astype(jnp.bfloat16)

def reference(clip_tokens, spatial_qkv, spatial_out, temporal_qkv, temporal_out, mlp_up, mlp_down):
    mixed = lax.map(lambda frame_rows: spatial_frame(frame_rows, spatial_qkv, spatial_out), clip_tokens)
    blocks = mixed.reshape(FRAMES, PATCHES // PATCH_DEV, PATCH_DEV, D).transpose(1, 0, 2, 3)

    def one_block(tokens):
        after_time = temporal_block(tokens, temporal_qkv, temporal_out)
        return feed_forward(after_time, mlp_up, mlp_down).reshape(FRAMES, PATCH_DEV, D)
    finished = lax.map(one_block, blocks)
    return finished.transpose(1, 0, 2, 3).reshape(FRAMES, PATCHES, D)
```

```python
import functools

import jax
import jax.numpy as jnp
from jax import lax
from jax.experimental import pallas as pl
from jax.experimental.pallas import tpu as pltpu
from jax.sharding import PartitionSpec as P

HEADS = 8
LANES = 128
BF16 = jnp.bfloat16
F32 = jnp.float32
VMEM_LIMIT = 48 * 1024 * 1024


def norm_rows(values):
    center = values - jnp.mean(values, axis=-1, keepdims=True)
    spread = jnp.mean(center * center, axis=-1, keepdims=True)
    return (center * lax.rsqrt(spread + 1e-05)).astype(BF16)


def attend_block(packed_ref, heads_ref, start, block, stride, width):
    rows = packed_ref.shape[0]
    head = width // HEADS
    pair = 2 * head
    scale = head ** (-0.5) * 1.4426950408889634
    low_q = lax.broadcasted_iota(jnp.int32, (block, pair), 1) < head
    low_v = lax.broadcasted_iota(jnp.int32, (rows, pair), 1) < head
    ones = jnp.concatenate(
        [jnp.where(low_v, 1.0, 0.0), jnp.where(low_v, 0.0, 1.0)], axis=0
    ).astype(BF16)
    if stride:
        query_at = start + lax.broadcasted_iota(jnp.int32, (2 * block, rows), 0)
        key_at = lax.broadcasted_iota(jnp.int32, (2 * block, rows), 1)
        same = lax.rem(query_at, stride) == lax.rem(key_at, stride)
    for at in range(0, width, pair):
        query = packed_ref[pl.ds(start, block), at : at + pair]
        key = packed_ref[:, width + at : width + at + pair]
        value = packed_ref[:, 2 * width + at : 2 * width + at + pair]
        zero_q = jnp.zeros_like(query)
        both = jnp.concatenate(
            [jnp.where(low_q, query, zero_q), jnp.where(low_q, zero_q, query)], axis=0
        )
        scores = lax.dot_general(both, key, (((1,), (1,)), ((), ())), preferred_element_type=F32)
        if stride:
            scores = jnp.where(same, scores, -jnp.inf)
        top = jnp.max(scores, axis=-1, keepdims=True)
        raised = jnp.exp2((scores - top) * scale).astype(BF16)
        side = jnp.concatenate([raised[:block], raised[block:]], axis=1)
        zero_v = jnp.zeros_like(value)
        values = jnp.concatenate(
            [jnp.where(low_v, value, zero_v), jnp.where(low_v, zero_v, value)], axis=0
        )
        total = jnp.dot(
            side, jnp.concatenate([values, ones], axis=1), preferred_element_type=F32
        )
        heads_ref[pl.ds(start, block), at : at + pair] = (
            total[:, :pair] / total[:, pair:]
        ).astype(BF16)


def attention_kernel(stride, x_ref, qkv_ref, out_ref, y_ref, packed_ref, heads_ref):
    rows, width = x_ref.shape
    normed = norm_rows(x_ref[...].astype(F32))
    packed_ref[...] = jnp.dot(normed, qkv_ref[...], preferred_element_type=F32).astype(BF16)
    block = min(rows, LANES)
    if rows == block:
        attend_block(packed_ref, heads_ref, 0, block, stride, width)
    else:

        @pl.loop(0, rows // block)
        def _(index):
            start = pl.multiple_of(index * block, block)
            attend_block(packed_ref, heads_ref, start, block, stride, width)

    y_ref[...] = (
        x_ref[...].astype(F32)
        + jnp.dot(heads_ref[...], out_ref[...], preferred_element_type=F32)
    ).astype(BF16)


def attention_layer(rows, w_qkv, w_out, stride):
    count, width = rows.shape
    return pl.pallas_call(
        functools.partial(attention_kernel, stride),
        out_shape=jax.ShapeDtypeStruct((count, width), BF16),
        in_specs=[pl.BlockSpec(memory_space=pltpu.VMEM)] * 3,
        out_specs=pl.BlockSpec(memory_space=pltpu.VMEM),
        scratch_shapes=[
            pltpu.VMEM((count, 3 * width), BF16),
            pltpu.VMEM((count, width), BF16),
        ],
        compiler_params=pltpu.CompilerParams(vmem_limit_bytes=VMEM_LIMIT),
    )(rows, w_qkv, w_out)


def mlp_block(x, up_ref, down_ref, piece):
    normed = norm_rows(x.astype(F32))
    total = x.astype(F32)
    for at in range(0, up_ref.shape[1], piece):
        u = jnp.dot(normed, up_ref[:, at : at + piece], preferred_element_type=F32)
        half = 0.5 * u
        bend = jnp.tanh(u * (0.7978845608028654 + 0.035677408136300125 * (u * u)))
        hidden = (half + half * bend).astype(BF16)
        total += jnp.dot(hidden, down_ref[at : at + piece, :], preferred_element_type=F32)
    return total.astype(BF16)


def mlp_kernel(x_ref, up_ref, down_ref, y_ref):
    rows = x_ref.shape[0]
    block = min(rows, LANES)
    piece = min(512, up_ref.shape[1])
    if rows == block:
        y_ref[...] = mlp_block(x_ref[...], up_ref, down_ref, piece)
    else:

        @pl.loop(0, rows // block)
        def _(index):
            here = pl.ds(pl.multiple_of(index * block, block), block)
            y_ref[here, :] = mlp_block(x_ref[here, :], up_ref, down_ref, piece)


def mlp_layer(rows, w_up, w_down):
    return pl.pallas_call(
        mlp_kernel,
        out_shape=jax.ShapeDtypeStruct(rows.shape, BF16),
        in_specs=[pl.BlockSpec(memory_space=pltpu.VMEM)] * 3,
        out_specs=pl.BlockSpec(memory_space=pltpu.VMEM),
        compiler_params=pltpu.CompilerParams(vmem_limit_bytes=VMEM_LIMIT),
    )(rows, w_up, w_down)


def local(clip_tokens, spatial_qkv, spatial_out, temporal_qkv, temporal_out, mlp_up, mlp_down):
    frame_count, patches, width = clip_tokens.shape
    devices = lax.axis_size("seq")
    share = patches // devices
    frames = frame_count * devices
    mixed = jnp.stack(
        [attention_layer(clip_tokens[i], spatial_qkv, spatial_out, 0) for i in range(frame_count)]
    )
    blocks = mixed.reshape(frame_count, devices, share, width)
    arrived = lax.all_to_all(blocks, "seq", split_axis=1, concat_axis=0, tiled=True)
    tokens = arrived.reshape(frames * share, width)
    after_time = attention_layer(tokens, temporal_qkv, temporal_out, share)
    returned = after_time.reshape(frames, 1, share, width)
    back = lax.all_to_all(returned, "seq", split_axis=0, concat_axis=1, tiled=True)
    result = mlp_layer(back.reshape(frame_count * patches, width), mlp_up, mlp_down)
    return result.reshape(frame_count, patches, width)


def solution(mesh):
    in_specs = (P(("groups", "seq"), None, None), P(), P(), P(), P(), P(), P())
    out_specs = P(("groups", "seq"), None, None)
    return jax.shard_map(local, mesh=mesh, in_specs=in_specs, out_specs=out_specs, check_vma=False)
```

```python
import functools

import jax
import jax.numpy as jnp
from jax import lax
from jax.experimental import pallas as pl
from jax.experimental.pallas import tpu as pltpu
from jax.sharding import PartitionSpec as P

HEADS = 8
LANES = 128
BF16 = jnp.bfloat16
F32 = jnp.float32
MIB = 1024 * 1024


def vmem_limit(rows):
    return 10 * MIB + rows * 32 * 1024


def norm_rows(values):
    center = values - jnp.mean(values, axis=-1, keepdims=True)
    spread = jnp.mean(center * center, axis=-1, keepdims=True)
    return (center * lax.rsqrt(spread + 1e-05)).astype(BF16)


def attend_block(packed_ref, heads_ref, start, block, stride, width):
    rows = packed_ref.shape[0]
    head = width // HEADS
    pair = 2 * head
    scale = head ** (-0.5) * 1.4426950408889634
    low_q = lax.broadcasted_iota(jnp.int32, (block, pair), 1) < head
    low_v = lax.broadcasted_iota(jnp.int32, (rows, pair), 1) < head
    ones = jnp.concatenate(
        [jnp.where(low_v, 1.0, 0.0), jnp.where(low_v, 0.0, 1.0)], axis=0
    ).astype(BF16)
    if stride:
        query_at = start + lax.broadcasted_iota(jnp.int32, (2 * block, rows), 0)
        key_at = lax.broadcasted_iota(jnp.int32, (2 * block, rows), 1)
        same = lax.rem(query_at, stride) == lax.rem(key_at, stride)
    for at in range(0, width, pair):
        query = packed_ref[pl.ds(start, block), at : at + pair]
        key = packed_ref[:, width + at : width + at + pair]
        value = packed_ref[:, 2 * width + at : 2 * width + at + pair]
        zero_q = jnp.zeros_like(query)
        both = jnp.concatenate(
            [jnp.where(low_q, query, zero_q), jnp.where(low_q, zero_q, query)], axis=0
        )
        scores = lax.dot_general(both, key, (((1,), (1,)), ((), ())), preferred_element_type=F32)
        if stride:
            scores = jnp.where(same, scores, -jnp.inf)
        top = jnp.max(scores, axis=-1, keepdims=True)
        raised = jnp.exp2((scores - top) * scale).astype(BF16)
        side = jnp.concatenate([raised[:block], raised[block:]], axis=1)
        zero_v = jnp.zeros_like(value)
        values = jnp.concatenate(
            [jnp.where(low_v, value, zero_v), jnp.where(low_v, zero_v, value)], axis=0
        )
        total = jnp.dot(
            side, jnp.concatenate([values, ones], axis=1), preferred_element_type=F32
        )
        heads_ref[pl.ds(start, block), at : at + pair] = (
            total[:, :pair] / total[:, pair:]
        ).astype(BF16)


def attend_rows(stride, x_ref, out_ref, y_ref, packed_ref, heads_ref):
    rows, width = x_ref.shape
    block = min(rows, LANES)
    if rows == block:
        attend_block(packed_ref, heads_ref, 0, block, stride, width)
    else:

        @pl.loop(0, rows // block)
        def _(index):
            start = pl.multiple_of(index * block, block)
            attend_block(packed_ref, heads_ref, start, block, stride, width)

    y_ref[...] = (
        x_ref[...].astype(F32)
        + jnp.dot(heads_ref[...], out_ref[...], preferred_element_type=F32)
    ).astype(BF16)


def spatial_kernel(
    x_hbm, qkv_hbm, out_hbm, next_qkv_hbm, next_out_hbm,
    y_ref, next_qkv_ref, next_out_ref,
    x_ref, qkv_ref, out_ref, packed_ref, heads_ref, sems,
):
    width = x_ref.shape[1]
    fetch_x = pltpu.make_async_copy(x_hbm, x_ref, sems.at[0])
    fetch_x.start()
    parts = []
    for part in range(3):
        columns = slice(part * width, (part + 1) * width)
        copy = pltpu.make_async_copy(
            qkv_hbm.at[:, columns], qkv_ref.at[:, columns], sems.at[part + 1]
        )
        copy.start()
        parts.append((columns, copy))
    fetch_out = pltpu.make_async_copy(out_hbm, out_ref, sems.at[4])
    fetch_out.start()
    fetch_next_qkv = pltpu.make_async_copy(next_qkv_hbm, next_qkv_ref, sems.at[5])
    fetch_next_qkv.start()
    fetch_next_out = pltpu.make_async_copy(next_out_hbm, next_out_ref, sems.at[6])
    fetch_next_out.start()
    fetch_x.wait()
    normed = norm_rows(x_ref[...].astype(F32))
    for columns, copy in parts:
        copy.wait()
        packed_ref[:, columns] = jnp.dot(
            normed, qkv_ref[:, columns], preferred_element_type=F32
        ).astype(BF16)
    fetch_out.wait()
    attend_rows(0, x_ref, out_ref, y_ref, packed_ref, heads_ref)
    fetch_next_qkv.wait()
    fetch_next_out.wait()


def spatial_layer(rows, w_qkv, w_out, next_qkv, next_out):
    count, width = rows.shape
    operands = (rows, w_qkv, w_out, next_qkv, next_out)
    return pl.pallas_call(
        spatial_kernel,
        out_shape=[
            jax.ShapeDtypeStruct((count, width), BF16),
            jax.ShapeDtypeStruct(next_qkv.shape, BF16),
            jax.ShapeDtypeStruct(next_out.shape, BF16),
        ],
        in_specs=[pl.BlockSpec(memory_space=pltpu.HBM)] * len(operands),
        out_specs=[pl.BlockSpec(memory_space=pltpu.VMEM)] * 3,
        scratch_shapes=[
            pltpu.VMEM(rows.shape, BF16),
            pltpu.VMEM(w_qkv.shape, BF16),
            pltpu.VMEM(w_out.shape, BF16),
            pltpu.VMEM((count, 3 * width), BF16),
            pltpu.VMEM((count, width), BF16),
            pltpu.SemaphoreType.DMA((7,)),
        ],
        compiler_params=pltpu.CompilerParams(vmem_limit_bytes=vmem_limit(count)),
    )(*(pltpu.with_memory_space_constraint(each, pltpu.HBM) for each in operands))


def temporal_kernel(stride, x_ref, qkv_ref, out_ref, y_ref, packed_ref, heads_ref):
    normed = norm_rows(x_ref[...].astype(F32))
    packed_ref[...] = jnp.dot(normed, qkv_ref[...], preferred_element_type=F32).astype(BF16)
    attend_rows(stride, x_ref, out_ref, y_ref, packed_ref, heads_ref)


def temporal_layer(rows, w_qkv, w_out, stride):
    count, width = rows.shape
    return pl.pallas_call(
        functools.partial(temporal_kernel, stride),
        out_shape=jax.ShapeDtypeStruct((count, width), BF16),
        in_specs=[pl.BlockSpec(memory_space=pltpu.VMEM)] * 3,
        out_specs=pl.BlockSpec(memory_space=pltpu.VMEM),
        scratch_shapes=[
            pltpu.VMEM((count, 3 * width), BF16),
            pltpu.VMEM((count, width), BF16),
        ],
        compiler_params=pltpu.CompilerParams(vmem_limit_bytes=vmem_limit(count)),
    )(rows, w_qkv, w_out)


def mlp_block(x, up_ref, down_ref, piece):
    normed = norm_rows(x.astype(F32))
    total = x.astype(F32)
    for at in range(0, up_ref.shape[1], piece):
        u = jnp.dot(normed, up_ref[:, at : at + piece], preferred_element_type=F32)
        half = 0.5 * u
        bend = jnp.tanh(u * (0.7978845608028654 + 0.035677408136300125 * (u * u)))
        hidden = (half + half * bend).astype(BF16)
        total += jnp.dot(hidden, down_ref[at : at + piece, :], preferred_element_type=F32)
    return total.astype(BF16)


def mlp_kernel(x_ref, up_ref, down_ref, y_ref):
    rows = x_ref.shape[0]
    block = min(rows, LANES)
    piece = min(512, up_ref.shape[1])
    if rows == block:
        y_ref[...] = mlp_block(x_ref[...], up_ref, down_ref, piece)
    else:

        @pl.loop(0, rows // block)
        def _(index):
            here = pl.ds(pl.multiple_of(index * block, block), block)
            y_ref[here, :] = mlp_block(x_ref[here, :], up_ref, down_ref, piece)


def mlp_layer(rows, w_up, w_down):
    return pl.pallas_call(
        mlp_kernel,
        out_shape=jax.ShapeDtypeStruct(rows.shape, BF16),
        in_specs=[pl.BlockSpec(memory_space=pltpu.VMEM)] * 3,
        out_specs=pl.BlockSpec(memory_space=pltpu.VMEM),
        compiler_params=pltpu.CompilerParams(vmem_limit_bytes=vmem_limit(rows.shape[0])),
    )(rows, w_up, w_down)


def local(clip_tokens, spatial_qkv, spatial_out, temporal_qkv, temporal_out, mlp_up, mlp_down):
    frame_count, patches, width = clip_tokens.shape
    devices = lax.axis_size("seq")
    share = patches // devices
    frames = frame_count * devices
    mixed = []
    for index in range(frame_count):
        rows, next_qkv, next_out = spatial_layer(
            clip_tokens[index], spatial_qkv, spatial_out, temporal_qkv, temporal_out
        )
        mixed.append(rows)
    mixed = jnp.stack(mixed)
    blocks = mixed.reshape(frame_count, devices, share, width)
    arrived = lax.all_to_all(blocks, "seq", split_axis=1, concat_axis=0, tiled=True)
    tokens = arrived.reshape(frames * share, width)
    after_time = temporal_layer(tokens, next_qkv, next_out, share)
    returned = after_time.reshape(frames, 1, share, width)
    back = lax.all_to_all(returned, "seq", split_axis=0, concat_axis=1, tiled=True)
    result = mlp_layer(back.reshape(frame_count * patches, width), mlp_up, mlp_down)
    return result.reshape(frame_count, patches, width)


def solution(mesh):
    in_specs = (P(("groups", "seq"), None, None), P(), P(), P(), P(), P(), P())
    out_specs = P(("groups", "seq"), None, None)
    return jax.shard_map(local, mesh=mesh, in_specs=in_specs, out_specs=out_specs, check_vma=False)
```

```python
import functools

import jax
import jax.numpy as jnp
from jax import lax
from jax.experimental import pallas as pl
from jax.experimental.pallas import tpu as pltpu
from jax.sharding import PartitionSpec as P

HEADS = 8
LANES = 128
SUBLANES = 8
BF16 = jnp.bfloat16
F32 = jnp.float32
MIB = 1024 * 1024


def vmem_limit(rows):
    return 10 * MIB + rows * 32 * 1024


def params(rows):
    return pltpu.CompilerParams(vmem_limit_bytes=vmem_limit(rows))


def in_hbm(*arrays):
    return tuple(pltpu.with_memory_space_constraint(each, pltpu.HBM) for each in arrays)


def vmem(count):
    return [pl.BlockSpec(memory_space=pltpu.VMEM)] * count


def norm_rows(values):
    center = values - jnp.mean(values, axis=-1, keepdims=True)
    spread = jnp.mean(center * center, axis=-1, keepdims=True)
    return (center * lax.rsqrt(spread + 1e-05)).astype(BF16)


def dot(left, right):
    return jnp.dot(left, right, preferred_element_type=F32)


def pair_ones(keys, head):
    low = lax.broadcasted_iota(jnp.int32, (keys, 2 * head), 1) < head
    return jnp.concatenate(
        [jnp.where(low, 1.0, 0.0), jnp.where(low, 0.0, 1.0)], axis=0
    ).astype(BF16)


def attend_pair(query, key, value, ones, same):
    block, pair = query.shape
    head = pair // 2
    scale = head ** (-0.5) * 1.4426950408889634
    low_q = lax.broadcasted_iota(jnp.int32, query.shape, 1) < head
    low_v = lax.broadcasted_iota(jnp.int32, value.shape, 1) < head
    zero_q, zero_v = jnp.zeros_like(query), jnp.zeros_like(value)
    both = jnp.concatenate(
        [jnp.where(low_q, query, zero_q), jnp.where(low_q, zero_q, query)], axis=0
    )
    scores = lax.dot_general(both, key, (((1,), (1,)), ((), ())), preferred_element_type=F32)
    if same is not None:
        scores = jnp.where(same, scores, -jnp.inf)
    top = jnp.max(scores, axis=-1, keepdims=True)
    raised = jnp.exp2((scores - top) * scale).astype(BF16)
    side = jnp.concatenate([raised[:block], raised[block:]], axis=1)
    values = jnp.concatenate(
        [jnp.where(low_v, value, zero_v), jnp.where(low_v, zero_v, value)], axis=0
    )
    total = dot(side, jnp.concatenate([values, ones], axis=1))
    return (total[:, :pair] / total[:, pair:]).astype(BF16)


def same_modulo(queries, keys, stride, start=0):
    query_at = start + lax.broadcasted_iota(jnp.int32, (2 * queries, keys), 0)
    key_at = lax.broadcasted_iota(jnp.int32, (2 * queries, keys), 1)
    return lax.rem(query_at, stride) == lax.rem(key_at, stride)


def attend_rows(packed_ref, heads_ref, stride):
    rows, width = heads_ref.shape
    pair = 2 * (width // HEADS)
    block = min(rows, LANES)
    ones = pair_ones(rows, pair // 2)

    def one_block(start):
        same = same_modulo(block, rows, stride, start) if stride else None
        for at in range(0, width, pair):
            heads_ref[pl.ds(start, block), at : at + pair] = attend_pair(
                packed_ref[pl.ds(start, block), at : at + pair],
                packed_ref[:, width + at : width + at + pair],
                packed_ref[:, 2 * width + at : 2 * width + at + pair],
                ones,
                same,
            )

    if rows == block:
        one_block(0)
    else:

        @pl.loop(0, rows // block)
        def _(index):
            one_block(pl.multiple_of(index * block, block))


def blocks_by_distance(x_ref, chips):
    size = x_ref.shape[0] // chips
    mine = lax.axis_index("seq") // 2
    return jnp.concatenate(
        [
            x_ref[pl.ds(pl.multiple_of((mine ^ distance) * size, size), size), :]
            for distance in range(chips)
        ],
        axis=0,
    )


def split_near(rows, chips):
    size = rows.shape[0] // chips
    parts = [rows[at * size : (at + 1) * size] for at in range(chips)]
    return jnp.concatenate(parts[0::2], axis=0), jnp.concatenate(parts[1::2], axis=0)


def spatial_kernel(
    chips,
    x_hbm, qkv_hbm, out_hbm, next_qkv_hbm, next_out_hbm,
    *refs,
):
    y_refs, refs = (refs[:2], refs[2:]) if chips else (refs[:1], refs[1:])
    next_qkv_ref, next_out_ref, x_ref, qkv_ref, out_ref, packed_ref, heads_ref, sems = refs
    width = x_ref.shape[1]
    fetch_x = pltpu.make_async_copy(x_hbm, x_ref, sems.at[0])
    fetch_x.start()
    parts = []
    for part in range(3):
        columns = slice(part * width, (part + 1) * width)
        copy = pltpu.make_async_copy(
            qkv_hbm.at[:, columns], qkv_ref.at[:, columns], sems.at[part + 1]
        )
        copy.start()
        parts.append((columns, copy))
    fetch_out = pltpu.make_async_copy(out_hbm, out_ref, sems.at[4])
    fetch_out.start()
    fetch_next_qkv = pltpu.make_async_copy(next_qkv_hbm, next_qkv_ref, sems.at[5])
    fetch_next_qkv.start()
    fetch_next_out = pltpu.make_async_copy(next_out_hbm, next_out_ref, sems.at[6])
    fetch_next_out.start()
    fetch_x.wait()
    x = blocks_by_distance(x_ref, chips) if chips else x_ref[...]
    normed = norm_rows(x.astype(F32))
    for columns, copy in parts:
        copy.wait()
        packed_ref[:, columns] = dot(normed, qkv_ref[:, columns]).astype(BF16)
    attend_rows(packed_ref, heads_ref, 0)
    fetch_out.wait()
    y = (x.astype(F32) + dot(heads_ref[...], out_ref[...])).astype(BF16)
    if chips:
        y_refs[0][...], y_refs[1][...] = split_near(y, chips)
    else:
        y_refs[0][...] = y
    fetch_next_qkv.wait()
    fetch_next_out.wait()


def spatial_layer(rows, w_qkv, w_out, next_qkv, next_out, chips):
    count, width = rows.shape
    halves = 2 if chips else 1
    return pl.pallas_call(
        functools.partial(spatial_kernel, chips),
        out_shape=[jax.ShapeDtypeStruct((count // halves, width), BF16)] * halves
        + [
            jax.ShapeDtypeStruct(next_qkv.shape, BF16),
            jax.ShapeDtypeStruct(next_out.shape, BF16),
        ],
        in_specs=[pl.BlockSpec(memory_space=pltpu.HBM)] * 5,
        out_specs=vmem(halves + 2),
        scratch_shapes=[
            pltpu.VMEM(rows.shape, BF16),
            pltpu.VMEM(w_qkv.shape, BF16),
            pltpu.VMEM(w_out.shape, BF16),
            pltpu.VMEM((count, 3 * width), BF16),
            pltpu.VMEM((count, width), BF16),
            pltpu.SemaphoreType.DMA((7,)),
        ],
        compiler_params=params(count),
    )(*in_hbm(rows, w_qkv, w_out, next_qkv, next_out))


def temporal_kernel(stride, x_ref, qkv_ref, out_ref, y_ref, packed_ref, heads_ref):
    normed = norm_rows(x_ref[...].astype(F32))
    packed_ref[...] = dot(normed, qkv_ref[...]).astype(BF16)
    attend_rows(packed_ref, heads_ref, stride)
    y_ref[...] = (x_ref[...].astype(F32) + dot(heads_ref[...], out_ref[...])).astype(BF16)


def temporal_layer(rows, w_qkv, w_out, stride):
    count, width = rows.shape
    return pl.pallas_call(
        functools.partial(temporal_kernel, stride),
        out_shape=jax.ShapeDtypeStruct((count, width), BF16),
        in_specs=vmem(3),
        out_specs=vmem(1)[0],
        scratch_shapes=[
            pltpu.VMEM((count, 3 * width), BF16),
            pltpu.VMEM((count, width), BF16),
        ],
        compiler_params=params(count),
    )(rows, w_qkv, w_out)


def by_patch_group(values, size):
    groups = size // SUBLANES
    frames = values.shape[0] // size
    return jnp.concatenate(
        [
            values[frame * size + group * SUBLANES : frame * size + (group + 1) * SUBLANES]
            for group in range(groups)
            for frame in range(frames)
        ],
        axis=0,
    )


def by_frame(values, size):
    groups = size // SUBLANES
    frames = values.shape[0] // size
    return jnp.concatenate(
        [
            values[(group * frames + frame) * SUBLANES : (group * frames + frame + 1) * SUBLANES]
            for frame in range(frames)
            for group in range(groups)
        ],
        axis=0,
    )


def normed_groups(x, size):
    x = x.astype(F32)
    center = x - jnp.mean(x, axis=-1, keepdims=True)
    spread = jnp.mean(center * center, axis=-1, keepdims=True)
    return by_patch_group(center * lax.rsqrt(spread + 1e-05), size).astype(BF16)


def project_kernel(size, x_ref, qkv_ref, packed_ref):
    packed_ref[...] = dot(normed_groups(x_ref[...], size), qkv_ref[...]).astype(BF16)


def project_own(rows, w_qkv, size):
    count, width = rows.shape
    return pl.pallas_call(
        functools.partial(project_kernel, size),
        out_shape=jax.ShapeDtypeStruct((count, w_qkv.shape[1]), BF16),
        in_specs=vmem(2),
        out_specs=vmem(1)[0],
        compiler_params=params(count),
        cost_estimate=pl.CostEstimate(
            flops=2 * count * width * w_qkv.shape[1],
            bytes_accessed=2 * (rows.size + w_qkv.size + count * w_qkv.shape[1]),
            transcendentals=0,
        ),
    )(rows, w_qkv)


def shared_kernel(size, chips, x_ref, packed_ref, other_ref, qkv_ref, out_ref, keep_ref, send_ref, heads_ref):
    count, width = x_ref.shape
    pair = 2 * (width // HEADS)
    other = dot(normed_groups(other_ref[...], size), qkv_ref[:, width:]).astype(BF16)
    groups = size // SUBLANES
    block = count // groups
    ones = pair_ones(2 * block, pair // 2)
    same = same_modulo(block, 2 * block, SUBLANES)
    for at in range(0, width, pair):
        for group in range(groups):
            here = slice(group * block, (group + 1) * block)
            key, value = (
                jnp.concatenate(
                    [packed_ref[here, skip + at : skip + at + pair],
                     other[here, skip - width + at : skip - width + at + pair]],
                    axis=0,
                )
                for skip in (width, 2 * width)
            )
            heads_ref[here, at : at + pair] = attend_pair(
                packed_ref[here, at : at + pair], key, value, ones, same
            )
    merged = by_frame(dot(heads_ref[...], out_ref[...]), size)
    y = (x_ref[...].astype(F32) + merged).astype(BF16)
    keep_ref[...], send_ref[...] = split_near(y, chips)


def shared_layer(rows, packed, other, w_qkv, w_out, size, chips):
    count, width = rows.shape
    return pl.pallas_call(
        functools.partial(shared_kernel, size, chips),
        out_shape=[jax.ShapeDtypeStruct((count // 2, width), BF16)] * 2,
        in_specs=vmem(5),
        out_specs=vmem(2),
        scratch_shapes=[pltpu.VMEM((count, width), BF16)],
        compiler_params=params(count),
    )(rows, packed, other, w_qkv, w_out)


def mlp_block(x, up_ref, down_ref):
    normed = norm_rows(x.astype(F32))
    u = dot(normed, up_ref[...])
    half = 0.5 * u
    bend = jnp.tanh(u * (0.7978845608028654 + 0.035677408136300125 * (u * u)))
    hidden = (half + half * bend).astype(BF16)
    return (x.astype(F32) + dot(hidden, down_ref[...])).astype(BF16)


def mlp_kernel(x_ref, up_ref, down_ref, y_ref):
    rows = x_ref.shape[0]
    block = min(rows, LANES)

    @pl.loop(0, rows // block)
    def _(index):
        here = pl.ds(pl.multiple_of(index * block, block), block)
        y_ref[here, :] = mlp_block(x_ref[here, :], up_ref, down_ref)


def mlp_layer(rows, w_up, w_down):
    return pl.pallas_call(
        mlp_kernel,
        out_shape=jax.ShapeDtypeStruct(rows.shape, BF16),
        in_specs=vmem(3),
        out_specs=vmem(1)[0],
        compiler_params=params(rows.shape[0]),
    )(rows, w_up, w_down)


def mlp_parts_kernel(chips, *refs):
    part_refs, (up_ref, down_ref, y_ref) = refs[:-3], refs[-3:]
    y = mlp_block(jnp.concatenate([each[...] for each in part_refs], axis=0), up_ref, down_ref)
    size = y.shape[0] // chips
    mine = lax.axis_index("seq") // 2
    for distance in range(chips):
        here = pl.ds(pl.multiple_of((mine ^ distance) * size, size), size)
        y_ref[here, :] = y[distance * size : (distance + 1) * size]


def mlp_parts_layer(parts, w_up, w_down, chips):
    count = sum(each.shape[0] for each in parts)
    return pl.pallas_call(
        functools.partial(mlp_parts_kernel, chips),
        out_shape=jax.ShapeDtypeStruct((count, parts[0].shape[1]), BF16),
        in_specs=vmem(len(parts) + 2),
        out_specs=vmem(1)[0],
        compiler_params=params(count),
    )(*parts, w_up, w_down)


def swap(rows, distance):
    pairs = [(at, at ^ distance) for at in range(lax.axis_size("seq"))]
    return lax.ppermute(rows, "seq", pairs)


def exchange(keep, send, far):
    got = swap(send, 2)
    size = keep.shape[0] // far

    def both(at):
        here = slice(at * size, (at + 1) * size)
        return jnp.concatenate([keep[here], got[here]], axis=0)

    arrived = {at: swap(both(at), 4 * at) for at in range(far - 1, 0, -1)}
    return [both(0)] + [arrived[at] for at in range(1, far)]


def by_permutes(tokens, spatial_qkv, spatial_out, temporal_qkv, temporal_out, mlp_up, mlp_down):
    devices = lax.axis_size("seq")
    chips, far = devices // 2, devices // 4
    size = tokens.shape[0] // chips
    keep, send, next_qkv, next_out = spatial_layer(
        tokens, spatial_qkv, spatial_out, temporal_qkv, temporal_out, chips
    )
    own = jnp.concatenate(exchange(keep, send, far), axis=0)
    other = swap(own, 1)
    packed = project_own(own, next_qkv, size)
    keep, send = shared_layer(own, packed, other, next_qkv, next_out, size, chips)
    return mlp_parts_layer(exchange(keep, send, far), mlp_up, mlp_down, chips)


def by_all_to_all(clip_tokens, spatial_qkv, spatial_out, temporal_qkv, temporal_out, mlp_up, mlp_down):
    frame_count, patches, width = clip_tokens.shape
    devices = lax.axis_size("seq")
    share = patches // devices
    frames = frame_count * devices
    mixed = []
    for index in range(frame_count):
        rows, next_qkv, next_out = spatial_layer(
            clip_tokens[index], spatial_qkv, spatial_out, temporal_qkv, temporal_out, 0
        )
        mixed.append(rows)
    blocks = jnp.stack(mixed).reshape(frame_count, devices, share, width)
    arrived = lax.all_to_all(blocks, "seq", split_axis=1, concat_axis=0, tiled=True)
    tokens = arrived.reshape(frames * share, width)
    after_time = temporal_layer(tokens, next_qkv, next_out, share)
    returned = after_time.reshape(frames, 1, share, width)
    back = lax.all_to_all(returned, "seq", split_axis=0, concat_axis=1, tiled=True)
    return mlp_layer(back.reshape(frame_count * patches, width), mlp_up, mlp_down)


def local(clip_tokens, *weights):
    frame_count, patches, width = clip_tokens.shape
    devices = lax.axis_size("seq")
    if (
        frame_count == 1
        and devices in (4, 8, 16)
        and patches % (SUBLANES * devices) == 0
        and patches <= LANES
    ):
        result = by_permutes(clip_tokens.reshape(patches, width), *weights)
    else:
        result = by_all_to_all(clip_tokens, *weights)
    return result.reshape(frame_count, patches, width)


def solution(mesh):
    in_specs = (P(("groups", "seq"), None, None), P(), P(), P(), P(), P(), P())
    out_specs = P(("groups", "seq"), None, None)
    return jax.shard_map(local, mesh=mesh, in_specs=in_specs, out_specs=out_specs, check_vma=False)
```

```python
import functools

import jax
import jax.numpy as jnp
from jax import lax
from jax.experimental import pallas as pl
from jax.experimental.pallas import tpu as pltpu
from jax.sharding import PartitionSpec as P

HEADS = 8
LANES = 128
BF16 = jnp.bfloat16
F32 = jnp.float32
MIB = 1024 * 1024


def vmem_limit(rows):
    return 10 * MIB + rows * 32 * 1024


def params(rows):
    return pltpu.CompilerParams(vmem_limit_bytes=vmem_limit(rows))


def in_hbm(*arrays):
    return tuple(pltpu.with_memory_space_constraint(each, pltpu.HBM) for each in arrays)


def vmem(count):
    return [pl.BlockSpec(memory_space=pltpu.VMEM)] * count


def norm_rows(values):
    center = values - jnp.mean(values, axis=-1, keepdims=True)
    spread = jnp.mean(center * center, axis=-1, keepdims=True)
    return (center * lax.rsqrt(spread + 1e-05)).astype(BF16)


def dot(left, right):
    return jnp.dot(left, right, preferred_element_type=F32)


def pair_ones(keys, head):
    low = lax.broadcasted_iota(jnp.int32, (keys, 2 * head), 1) < head
    return jnp.concatenate(
        [jnp.where(low, 1.0, 0.0), jnp.where(low, 0.0, 1.0)], axis=0
    ).astype(BF16)


def attend_heads(query, key, value, ones, same):
    block, width = query.shape
    head = width // HEADS
    pair = 2 * head
    scale = head ** (-0.5) * 1.4426950408889634
    low_q = lax.broadcasted_iota(jnp.int32, (block, pair), 1) < head
    low_v = lax.broadcasted_iota(jnp.int32, (value.shape[0], pair), 1) < head

    def split(part, low):
        zero = jnp.zeros_like(part)
        return jnp.concatenate([jnp.where(low, part, zero), jnp.where(low, zero, part)], axis=0)

    heads = []
    for at in range(0, width, pair):
        here = slice(at, at + pair)
        scores = lax.dot_general(
            split(query[:, here], low_q), key[:, here], (((1,), (1,)), ((), ())),
            preferred_element_type=F32,
        )
        if same is not None:
            scores = jnp.where(same, scores, -jnp.inf)
        top = jnp.max(scores, axis=-1, keepdims=True)
        raised = jnp.exp2((scores - top) * scale).astype(BF16)
        side = jnp.concatenate([raised[:block], raised[block:]], axis=1)
        total = dot(side, jnp.concatenate([split(value[:, here], low_v), ones], axis=1))
        heads.append((total[:, :pair] / total[:, pair:]).astype(BF16))
    return jnp.concatenate(heads, axis=1)


def same_modulo(queries, keys, stride, start=0):
    query_at = start + lax.broadcasted_iota(jnp.int32, (2 * queries, keys), 0)
    key_at = lax.broadcasted_iota(jnp.int32, (2 * queries, keys), 1)
    return lax.rem(query_at, stride) == lax.rem(key_at, stride)


def attend_and_project(packed, w_out, x, y_ref, heads_ref, stride):
    rows, width = y_ref.shape
    pair = 2 * (width // HEADS)
    block = min(rows, LANES)
    ones = pair_ones(rows, pair // 2)
    keys, values = packed[:, width : 2 * width], packed[:, 2 * width :]
    if rows == block:
        same = same_modulo(block, rows, stride) if stride else None
        heads = attend_heads(packed[:, :width], keys, values, ones, same)
        y_ref[...] = (x + dot(heads, w_out[...])).astype(BF16)
    else:

        @pl.loop(0, rows // block)
        def _(index):
            start = pl.multiple_of(index * block, block)
            here = pl.ds(start, block)
            same = same_modulo(block, rows, stride, start) if stride else None
            heads_ref[here, :] = attend_heads(packed[here, :width], keys, values, ones, same)

        y_ref[...] = (x + dot(heads_ref[...], w_out[...])).astype(BF16)


def spatial_kernel(
    x_hbm, qkv_hbm, out_hbm, next_qkv_hbm, next_out_hbm,
    y_ref, next_qkv_ref, next_out_ref,
    x_ref, qkv_ref, out_ref, packed_ref, heads_ref, sems,
):
    width = x_ref.shape[1]

    def fetch(source, target, at):
        copy = pltpu.make_async_copy(source, target, sems.at[at])
        copy.start()
        return copy

    x_copy = fetch(x_hbm, x_ref, 0)
    copies = []
    for block in range(3):
        columns = slice(block * width, (block + 1) * width)
        copies.append(fetch(qkv_hbm.at[:, columns], qkv_ref.at[:, columns], 1 + block))
    out_copy = fetch(out_hbm, out_ref, 4)
    next_copies = [
        fetch(next_qkv_hbm, next_qkv_ref, 5), fetch(next_out_hbm, next_out_ref, 6)
    ]
    x_copy.wait()
    x = x_ref[...].astype(F32)
    normed = norm_rows(x)
    for block, copy in enumerate(copies):
        columns = slice(block * width, (block + 1) * width)
        copy.wait()
        packed_ref[:, columns] = dot(normed, qkv_ref[:, columns]).astype(BF16)
    out_copy.wait()
    attend_and_project(packed_ref, out_ref, x, y_ref, heads_ref, 0)
    for copy in next_copies:
        copy.wait()


def spatial_layer(rows, w_qkv, w_out, next_qkv, next_out):
    count, width = rows.shape
    return pl.pallas_call(
        spatial_kernel,
        out_shape=[
            jax.ShapeDtypeStruct((count, width), BF16),
            jax.ShapeDtypeStruct(next_qkv.shape, BF16),
            jax.ShapeDtypeStruct(next_out.shape, BF16),
        ],
        in_specs=[pl.BlockSpec(memory_space=pltpu.HBM)] * 5,
        out_specs=vmem(3),
        scratch_shapes=[
            pltpu.VMEM(rows.shape, BF16),
            pltpu.VMEM(w_qkv.shape, BF16),
            pltpu.VMEM(w_out.shape, BF16),
            pltpu.VMEM((count, 3 * width), BF16),
            pltpu.VMEM((count, width), BF16),
            pltpu.SemaphoreType.DMA((7,)),
        ],
        compiler_params=params(count),
    )(*in_hbm(rows, w_qkv, w_out, next_qkv, next_out))


def temporal_kernel(stride, x_ref, qkv_ref, out_ref, y_ref, packed_ref, heads_ref):
    x = x_ref[...].astype(F32)
    packed = dot(norm_rows(x), qkv_ref[...]).astype(BF16)
    if x.shape[0] > LANES:
        packed_ref[...] = packed
        packed = packed_ref
    attend_and_project(packed, out_ref, x, y_ref, heads_ref, stride)


def temporal_layer(rows, w_qkv, w_out, stride):
    count, width = rows.shape
    return pl.pallas_call(
        functools.partial(temporal_kernel, stride),
        out_shape=jax.ShapeDtypeStruct((count, width), BF16),
        in_specs=vmem(3),
        out_specs=vmem(1)[0],
        scratch_shapes=[
            pltpu.VMEM((count, 3 * width), BF16),
            pltpu.VMEM((count, width), BF16),
        ],
        compiler_params=params(count),
    )(rows, w_qkv, w_out)


def mlp_block(x, up_ref, down_ref):
    normed = norm_rows(x.astype(F32))
    u = dot(normed, up_ref[...])
    half = 0.5 * u
    bend = jnp.tanh(u * (0.7978845608028654 + 0.035677408136300125 * (u * u)))
    hidden = (half + half * bend).astype(BF16)
    return (x.astype(F32) + dot(hidden, down_ref[...])).astype(BF16)


def mlp_kernel(x_ref, up_ref, down_ref, y_ref):
    rows = x_ref.shape[0]
    block = min(rows, LANES)

    @pl.loop(0, rows // block)
    def _(index):
        here = pl.ds(pl.multiple_of(index * block, block), block)
        y_ref[here, :] = mlp_block(x_ref[here, :], up_ref, down_ref)


def mlp_layer(rows, w_up, w_down):
    return pl.pallas_call(
        mlp_kernel,
        out_shape=jax.ShapeDtypeStruct(rows.shape, BF16),
        in_specs=vmem(3),
        out_specs=vmem(1)[0],
        compiler_params=params(rows.shape[0]),
    )(rows, w_up, w_down)


def local(clip_tokens, spatial_qkv, spatial_out, temporal_qkv, temporal_out, mlp_up, mlp_down):
    frame_count, patches, width = clip_tokens.shape
    devices = lax.axis_size("seq")
    share = patches // devices
    frames = frame_count * devices
    mixed = []
    for index in range(frame_count):
        rows, next_qkv, next_out = spatial_layer(
            clip_tokens[index], spatial_qkv, spatial_out, temporal_qkv, temporal_out
        )
        mixed.append(rows)
    mixed = jnp.stack(mixed)
    mixed, mlp_up, mlp_down = lax.optimization_barrier((mixed, mlp_up, mlp_down))
    blocks = mixed.reshape(frame_count, devices, share, width)
    arrived = lax.all_to_all(blocks, "seq", split_axis=1, concat_axis=0, tiled=True)
    tokens = arrived.reshape(frames * share, width)
    after_time = temporal_layer(tokens, next_qkv, next_out, share)
    returned = after_time.reshape(frames, 1, share, width)
    back = lax.all_to_all(returned, "seq", split_axis=0, concat_axis=1, tiled=True)
    result = mlp_layer(back.reshape(frame_count * patches, width), mlp_up, mlp_down)
    return result.reshape(frame_count, patches, width)


def solution(mesh):
    in_specs = (P(("groups", "seq"), None, None), P(), P(), P(), P(), P(), P())
    out_specs = P(("groups", "seq"), None, None)
    return jax.shard_map(local, mesh=mesh, in_specs=in_specs, out_specs=out_specs, check_vma=False)
```

```python
import functools

import jax
import jax.numpy as jnp
from jax import lax
from jax.experimental import pallas as pl
from jax.experimental.pallas import tpu as pltpu
from jax.sharding import PartitionSpec as P

HEADS = 8
LANES = 128
BF16 = jnp.bfloat16
F32 = jnp.float32
MIB = 1024 * 1024


def vmem_limit(rows):
    return 10 * MIB + rows * 32 * 1024


def params(rows):
    return pltpu.CompilerParams(vmem_limit_bytes=vmem_limit(rows))


def in_hbm(*arrays):
    return tuple(pltpu.with_memory_space_constraint(each, pltpu.HBM) for each in arrays)


def vmem(count):
    return [pl.BlockSpec(memory_space=pltpu.VMEM)] * count


def norm_rows(values):
    center = values - jnp.mean(values, axis=-1, keepdims=True)
    spread = jnp.mean(center * center, axis=-1, keepdims=True)
    return (center * lax.rsqrt(spread + 1e-05)).astype(BF16)


def dot(left, right):
    return jnp.dot(left, right, preferred_element_type=F32)


def pair_ones(keys, head):
    low = lax.broadcasted_iota(jnp.int32, (keys, 2 * head), 1) < head
    return jnp.concatenate(
        [jnp.where(low, 1.0, 0.0), jnp.where(low, 0.0, 1.0)], axis=0
    ).astype(BF16)


def attend_heads(query, key, value, ones, same):
    block, width = query.shape
    head = width // HEADS
    pair = 2 * head
    scale = head ** (-0.5) * 1.4426950408889634
    low_q = lax.broadcasted_iota(jnp.int32, (block, pair), 1) < head
    low_v = lax.broadcasted_iota(jnp.int32, (value.shape[0], pair), 1) < head

    def split(part, low):
        zero = jnp.zeros_like(part)
        return jnp.concatenate([jnp.where(low, part, zero), jnp.where(low, zero, part)], axis=0)

    heads = []
    for at in range(0, width, pair):
        here = slice(at, at + pair)
        scores = lax.dot_general(
            split(query[:, here], low_q), key[:, here], (((1,), (1,)), ((), ())),
            preferred_element_type=F32,
        )
        if same is not None:
            scores = jnp.where(same, scores, -jnp.inf)
        top = jnp.max(scores, axis=-1, keepdims=True)
        raised = jnp.exp2((scores - top) * scale).astype(BF16)
        side = jnp.concatenate([raised[:block], raised[block:]], axis=1)
        total = dot(side, jnp.concatenate([split(value[:, here], low_v), ones], axis=1))
        heads.append((total[:, :pair] / total[:, pair:]).astype(BF16))
    return jnp.concatenate(heads, axis=1)


def same_modulo(queries, keys, stride, start=0):
    query_at = start + lax.broadcasted_iota(jnp.int32, (2 * queries, keys), 0)
    key_at = lax.broadcasted_iota(jnp.int32, (2 * queries, keys), 1)
    return lax.rem(query_at, stride) == lax.rem(key_at, stride)


def attend_and_project(packed, w_out, x, y_ref, heads_ref, stride):
    rows, width = y_ref.shape
    pair = 2 * (width // HEADS)
    block = min(rows, LANES)
    ones = pair_ones(rows, pair // 2)
    keys, values = packed[:, width : 2 * width], packed[:, 2 * width :]
    if rows == block:
        same = same_modulo(block, rows, stride) if stride else None
        heads = attend_heads(packed[:, :width], keys, values, ones, same)
        y_ref[...] = (x + dot(heads, w_out[...])).astype(BF16)
    else:

        @pl.loop(0, rows // block)
        def _(index):
            start = pl.multiple_of(index * block, block)
            here = pl.ds(start, block)
            same = same_modulo(block, rows, stride, start) if stride else None
            heads_ref[here, :] = attend_heads(packed[here, :width], keys, values, ones, same)

        y_ref[...] = (x + dot(heads_ref[...], w_out[...])).astype(BF16)


def spatial_kernel(
    x_hbm, qkv_hbm, out_hbm, next_qkv_hbm, next_out_hbm,
    y_ref, next_qkv_ref, next_out_ref,
    x_ref, qkv_ref, out_ref, packed_ref, heads_ref, sems,
):
    width = x_ref.shape[1]

    def fetch(source, target, at):
        copy = pltpu.make_async_copy(source, target, sems.at[at])
        copy.start()
        return copy

    x_copy = fetch(x_hbm, x_ref, 0)
    copies = [
        fetch(qkv_hbm.at[:, : 2 * width], qkv_ref.at[:, : 2 * width], 1),
        fetch(qkv_hbm.at[:, 2 * width :], qkv_ref.at[:, 2 * width :], 2),
    ]
    out_copy = fetch(out_hbm, out_ref, 4)
    next_copies = [
        fetch(next_qkv_hbm, next_qkv_ref, 5), fetch(next_out_hbm, next_out_ref, 6)
    ]
    x_copy.wait()
    x = x_ref[...].astype(F32)
    normed = norm_rows(x)
    copies[0].wait()
    first = dot(normed, qkv_ref[:, : 2 * width]).astype(BF16)
    copies[1].wait()
    out_copy.wait()
    packed = jnp.concatenate([first, dot(normed, qkv_ref[:, 2 * width :]).astype(BF16)], axis=1)
    if x.shape[0] > LANES:
        packed_ref[...] = packed
        packed = packed_ref
    attend_and_project(packed, out_ref, x, y_ref, heads_ref, 0)
    for copy in next_copies:
        copy.wait()


def spatial_layer(rows, w_qkv, w_out, next_qkv, next_out):
    count, width = rows.shape
    return pl.pallas_call(
        spatial_kernel,
        out_shape=[
            jax.ShapeDtypeStruct((count, width), BF16),
            jax.ShapeDtypeStruct(next_qkv.shape, BF16),
            jax.ShapeDtypeStruct(next_out.shape, BF16),
        ],
        in_specs=[pl.BlockSpec(memory_space=pltpu.HBM)] * 5,
        out_specs=vmem(3),
        scratch_shapes=[
            pltpu.VMEM(rows.shape, BF16),
            pltpu.VMEM(w_qkv.shape, BF16),
            pltpu.VMEM(w_out.shape, BF16),
            pltpu.VMEM((count, 3 * width), BF16),
            pltpu.VMEM((count, width), BF16),
            pltpu.SemaphoreType.DMA((7,)),
        ],
        compiler_params=params(count),
    )(*in_hbm(rows, w_qkv, w_out, next_qkv, next_out))


def temporal_kernel(stride, x_ref, qkv_ref, out_ref, y_ref, packed_ref, heads_ref):
    x = x_ref[...].astype(F32)
    packed = dot(norm_rows(x), qkv_ref[...]).astype(BF16)
    if x.shape[0] > LANES:
        packed_ref[...] = packed
        packed = packed_ref
    attend_and_project(packed, out_ref, x, y_ref, heads_ref, stride)


def temporal_layer(rows, w_qkv, w_out, stride):
    count, width = rows.shape
    return pl.pallas_call(
        functools.partial(temporal_kernel, stride),
        out_shape=jax.ShapeDtypeStruct((count, width), BF16),
        in_specs=vmem(3),
        out_specs=vmem(1)[0],
        scratch_shapes=[
            pltpu.VMEM((count, 3 * width), BF16),
            pltpu.VMEM((count, width), BF16),
        ],
        compiler_params=params(count),
    )(rows, w_qkv, w_out)


def mlp_block(x, up_ref, down_ref):
    normed = norm_rows(x.astype(F32))
    u = dot(normed, up_ref[...])
    half = 0.5 * u
    bend = jnp.tanh(u * (0.7978845608028654 + 0.035677408136300125 * (u * u)))
    hidden = (half + half * bend).astype(BF16)
    return (x.astype(F32) + dot(hidden, down_ref[...])).astype(BF16)


def mlp_kernel(x_ref, up_ref, down_ref, y_ref):
    rows = x_ref.shape[0]
    block = min(rows, LANES)

    @pl.loop(0, rows // block)
    def _(index):
        here = pl.ds(pl.multiple_of(index * block, block), block)
        y_ref[here, :] = mlp_block(x_ref[here, :], up_ref, down_ref)


def mlp_layer(rows, w_up, w_down):
    return pl.pallas_call(
        mlp_kernel,
        out_shape=jax.ShapeDtypeStruct(rows.shape, BF16),
        in_specs=vmem(3),
        out_specs=vmem(1)[0],
        compiler_params=params(rows.shape[0]),
    )(rows, w_up, w_down)


def middle_first(devices):
    order = list(range(devices))
    middle = max(devices // 2 - 2, 0)
    order[0], order[middle] = order[middle], order[0]
    return order


def local(clip_tokens, spatial_qkv, spatial_out, temporal_qkv, temporal_out, mlp_up, mlp_down):
    frame_count, patches, width = clip_tokens.shape
    devices = lax.axis_size("seq")
    share = patches // devices
    frames = frame_count * devices
    order = middle_first(devices)
    mixed = []
    for index in range(frame_count):
        rows, next_qkv, next_out = spatial_layer(
            clip_tokens[index], spatial_qkv, spatial_out, temporal_qkv, temporal_out
        )
        mixed.append(rows)
    mixed = jnp.stack(mixed)
    mixed, mlp_up, mlp_down = lax.optimization_barrier((mixed, mlp_up, mlp_down))
    blocks = mixed.reshape(frame_count, devices, share, width)
    arrived = lax.all_to_all(
        blocks, "seq", split_axis=1, concat_axis=0, axis_index_groups=[order], tiled=True
    )
    tokens = arrived.reshape(frames * share, width)
    after_time = temporal_layer(tokens, next_qkv, next_out, share)
    returned = after_time.reshape(frames, 1, share, width)
    back = lax.all_to_all(
        returned, "seq", split_axis=0, concat_axis=1, axis_index_groups=[order], tiled=True
    )
    result = mlp_layer(back.reshape(frame_count * patches, width), mlp_up, mlp_down)
    return result.reshape(frame_count, patches, width)


def solution(mesh):
    in_specs = (P(("groups", "seq"), None, None), P(), P(), P(), P(), P(), P())
    out_specs = P(("groups", "seq"), None, None)
    return jax.shard_map(local, mesh=mesh, in_specs=in_specs, out_specs=out_specs, check_vma=False)
```

```python
import functools

import jax
import jax.numpy as jnp
import numpy as np
from jax import lax
from jax.experimental import pallas as pl
from jax.experimental.pallas import tpu as pltpu
from jax.sharding import PartitionSpec as P

HEADS = 8
LANES = 128
BF16 = jnp.bfloat16
F32 = jnp.float32
MIB = 1024 * 1024


def vmem_limit(rows):
    return 10 * MIB + rows * 32 * 1024


def params(rows):
    return pltpu.CompilerParams(vmem_limit_bytes=vmem_limit(rows))


def in_hbm(*arrays):
    return tuple(pltpu.with_memory_space_constraint(each, pltpu.HBM) for each in arrays)


def vmem(count):
    return [pl.BlockSpec(memory_space=pltpu.VMEM)] * count


def norm_rows(values):
    center = values - jnp.mean(values, axis=-1, keepdims=True)
    spread = jnp.mean(center * center, axis=-1, keepdims=True)
    return (center * lax.rsqrt(spread + 1e-05)).astype(BF16)


def dot(left, right):
    return jnp.dot(left, right, preferred_element_type=F32)


def pair_ones(keys, head):
    low = lax.broadcasted_iota(jnp.int32, (keys, 2 * head), 1) < head
    return jnp.concatenate(
        [jnp.where(low, 1.0, 0.0), jnp.where(low, 0.0, 1.0)], axis=0
    ).astype(BF16)


def attend_heads(query, key, value, ones, same):
    block, width = query.shape
    head = width // HEADS
    pair = 2 * head
    scale = head ** (-0.5) * 1.4426950408889634
    low_q = lax.broadcasted_iota(jnp.int32, (block, pair), 1) < head
    low_v = lax.broadcasted_iota(jnp.int32, (value.shape[0], pair), 1) < head

    def split(part, low):
        zero = jnp.zeros_like(part)
        return jnp.concatenate([jnp.where(low, part, zero), jnp.where(low, zero, part)], axis=0)

    heads = []
    for at in range(0, width, pair):
        here = slice(at, at + pair)
        scores = lax.dot_general(
            split(query[:, here], low_q), key[:, here], (((1,), (1,)), ((), ())),
            preferred_element_type=F32,
        )
        if same is not None:
            scores = jnp.where(same, scores, -jnp.inf)
        top = jnp.max(scores, axis=-1, keepdims=True)
        raised = jnp.exp2((scores - top) * scale).astype(BF16)
        side = jnp.concatenate([raised[:block], raised[block:]], axis=1)
        total = dot(side, jnp.concatenate([split(value[:, here], low_v), ones], axis=1))
        heads.append((total[:, :pair] / total[:, pair:]).astype(BF16))
    return jnp.concatenate(heads, axis=1)


def same_modulo(queries, keys, stride, start=0):
    query_at = start + lax.broadcasted_iota(jnp.int32, (2 * queries, keys), 0)
    key_at = lax.broadcasted_iota(jnp.int32, (2 * queries, keys), 1)
    return lax.rem(query_at, stride) == lax.rem(key_at, stride)


def attend_and_project(packed, w_out, x, y_ref, heads_ref, stride):
    rows, width = y_ref.shape
    pair = 2 * (width // HEADS)
    block = min(rows, LANES)
    ones = pair_ones(rows, pair // 2)
    keys, values = packed[:, width : 2 * width], packed[:, 2 * width :]
    if rows == block:
        same = same_modulo(block, rows, stride) if stride else None
        heads = attend_heads(packed[:, :width], keys, values, ones, same)
        y_ref[...] = (x + dot(heads, w_out[...])).astype(BF16)
    else:

        @pl.loop(0, rows // block)
        def _(index):
            start = pl.multiple_of(index * block, block)
            here = pl.ds(start, block)
            same = same_modulo(block, rows, stride, start) if stride else None
            heads_ref[here, :] = attend_heads(packed[here, :width], keys, values, ones, same)

        y_ref[...] = (x + dot(heads_ref[...], w_out[...])).astype(BF16)


def spatial_kernel(
    x_hbm, qkv_hbm, out_hbm, next_qkv_hbm, next_out_hbm,
    y_ref, next_qkv_ref, next_out_ref,
    x_ref, qkv_ref, out_ref, packed_ref, heads_ref, sems,
):
    width = x_ref.shape[1]

    def fetch(source, target, at):
        copy = pltpu.make_async_copy(source, target, sems.at[at])
        copy.start()
        return copy

    x_copy = fetch(x_hbm, x_ref, 0)
    copies = [
        fetch(qkv_hbm.at[:, : 2 * width], qkv_ref.at[:, : 2 * width], 1),
        fetch(qkv_hbm.at[:, 2 * width :], qkv_ref.at[:, 2 * width :], 2),
    ]
    out_copy = fetch(out_hbm, out_ref, 4)
    next_copies = [
        fetch(next_qkv_hbm, next_qkv_ref, 5), fetch(next_out_hbm, next_out_ref, 6)
    ]
    x_copy.wait()
    x = x_ref[...].astype(F32)
    normed = norm_rows(x)
    copies[0].wait()
    first = dot(normed, qkv_ref[:, : 2 * width]).astype(BF16)
    copies[1].wait()
    out_copy.wait()
    packed = jnp.concatenate([first, dot(normed, qkv_ref[:, 2 * width :]).astype(BF16)], axis=1)
    if x.shape[0] > LANES:
        packed_ref[...] = packed
        packed = packed_ref
    attend_and_project(packed, out_ref, x, y_ref, heads_ref, 0)
    for copy in next_copies:
        copy.wait()


def spatial_layer(rows, w_qkv, w_out, next_qkv, next_out):
    count, width = rows.shape
    return pl.pallas_call(
        spatial_kernel,
        out_shape=[
            jax.ShapeDtypeStruct((count, width), BF16),
            jax.ShapeDtypeStruct(next_qkv.shape, BF16),
            jax.ShapeDtypeStruct(next_out.shape, BF16),
        ],
        in_specs=[pl.BlockSpec(memory_space=pltpu.HBM)] * 5,
        out_specs=vmem(3),
        scratch_shapes=[
            pltpu.VMEM(rows.shape, BF16),
            pltpu.VMEM(w_qkv.shape, BF16),
            pltpu.VMEM(w_out.shape, BF16),
            pltpu.VMEM((count, 3 * width), BF16),
            pltpu.VMEM((count, width), BF16),
            pltpu.SemaphoreType.DMA((7,)),
        ],
        compiler_params=params(count),
    )(*in_hbm(rows, w_qkv, w_out, next_qkv, next_out))


def temporal_kernel(stride, x_ref, qkv_ref, out_ref, y_ref, packed_ref, heads_ref):
    x = x_ref[...].astype(F32)
    packed = dot(norm_rows(x), qkv_ref[...]).astype(BF16)
    if x.shape[0] > LANES:
        packed_ref[...] = packed
        packed = packed_ref
    attend_and_project(packed, out_ref, x, y_ref, heads_ref, stride)


def temporal_layer(rows, w_qkv, w_out, stride):
    count, width = rows.shape
    return pl.pallas_call(
        functools.partial(temporal_kernel, stride),
        out_shape=jax.ShapeDtypeStruct((count, width), BF16),
        in_specs=vmem(3),
        out_specs=vmem(1)[0],
        scratch_shapes=[
            pltpu.VMEM((count, 3 * width), BF16),
            pltpu.VMEM((count, width), BF16),
        ],
        compiler_params=params(count),
    )(rows, w_qkv, w_out)


def mlp_block(x, up_ref, down_ref):
    normed = norm_rows(x.astype(F32))
    u = dot(normed, up_ref[...])
    half = 0.5 * u
    bend = jnp.tanh(u * (0.7978845608028654 + 0.035677408136300125 * (u * u)))
    hidden = (half + half * bend).astype(BF16)
    return (x.astype(F32) + dot(hidden, down_ref[...])).astype(BF16)


def mlp_kernel(x_ref, up_ref, down_ref, y_ref):
    rows = x_ref.shape[0]
    block = min(rows, LANES)

    @pl.loop(0, rows // block)
    def _(index):
        here = pl.ds(pl.multiple_of(index * block, block), block)
        y_ref[here, :] = mlp_block(x_ref[here, :], up_ref, down_ref)


def mlp_layer(rows, w_up, w_down):
    return pl.pallas_call(
        mlp_kernel,
        out_shape=jax.ShapeDtypeStruct(rows.shape, BF16),
        in_specs=vmem(3),
        out_specs=vmem(1)[0],
        compiler_params=params(rows.shape[0]),
    )(rows, w_up, w_down)


def exchange_order(devices):
    order = np.random.RandomState(0).permutation(devices).tolist()
    first = order.index(min(devices // 2 + 3, devices - 1))
    order[0], order[first] = order[first], order[0]
    return order


def local(clip_tokens, spatial_qkv, spatial_out, temporal_qkv, temporal_out, mlp_up, mlp_down):
    frame_count, patches, width = clip_tokens.shape
    devices = lax.axis_size("seq")
    share = patches // devices
    frames = frame_count * devices
    order = exchange_order(devices)
    mixed = []
    for index in range(frame_count):
        rows, next_qkv, next_out = spatial_layer(
            clip_tokens[index], spatial_qkv, spatial_out, temporal_qkv, temporal_out
        )
        mixed.append(rows)
    mixed = jnp.stack(mixed)
    mixed, mlp_up, mlp_down = lax.optimization_barrier((mixed, mlp_up, mlp_down))
    blocks = mixed.reshape(frame_count, devices, share, width)
    arrived = lax.all_to_all(
        blocks, "seq", split_axis=1, concat_axis=0, axis_index_groups=[order], tiled=True
    )
    tokens = arrived.reshape(frames * share, width)
    after_time = temporal_layer(tokens, next_qkv, next_out, share)
    returned = after_time.reshape(frames, 1, share, width)
    back = lax.all_to_all(
        returned, "seq", split_axis=0, concat_axis=1, axis_index_groups=[order], tiled=True
    )
    result = mlp_layer(back.reshape(frame_count * patches, width), mlp_up, mlp_down)
    return result.reshape(frame_count, patches, width)


def solution(mesh):
    in_specs = (P(("groups", "seq"), None, None), P(), P(), P(), P(), P(), P())
    out_specs = P(("groups", "seq"), None, None)
    return jax.shard_map(local, mesh=mesh, in_specs=in_specs, out_specs=out_specs, check_vma=False)
```

```python
import functools

import jax
import jax.numpy as jnp
import numpy as np
from jax import lax
from jax.experimental import pallas as pl
from jax.experimental.pallas import tpu as pltpu
from jax.sharding import PartitionSpec as P

HEADS = 8
LANES = 128
BF16 = jnp.bfloat16
F32 = jnp.float32
MIB = 1024 * 1024


def vmem_limit(rows):
    return 10 * MIB + rows * 32 * 1024


def params(rows):
    return pltpu.CompilerParams(vmem_limit_bytes=vmem_limit(rows))


def in_hbm(*arrays):
    return tuple(pltpu.with_memory_space_constraint(each, pltpu.HBM) for each in arrays)


def vmem(count):
    return [pl.BlockSpec(memory_space=pltpu.VMEM)] * count


def norm_rows(values):
    center = values - jnp.mean(values, axis=-1, keepdims=True)
    spread = jnp.mean(center * center, axis=-1, keepdims=True)
    return (center * lax.rsqrt(spread + 1e-05)).astype(BF16)


def dot(left, right):
    return jnp.dot(left, right, preferred_element_type=F32)


def pair_ones(keys, head):
    low = lax.broadcasted_iota(jnp.int32, (keys, 2 * head), 1) < head
    return jnp.concatenate(
        [jnp.where(low, 1.0, 0.0), jnp.where(low, 0.0, 1.0)], axis=0
    ).astype(BF16)


def attend_heads(query, key, value, ones, same):
    block, width = query.shape
    head = width // HEADS
    pair = 2 * head
    scale = head ** (-0.5) * 1.4426950408889634
    low_q = lax.broadcasted_iota(jnp.int32, (block, pair), 1) < head
    low_v = lax.broadcasted_iota(jnp.int32, (value.shape[0], pair), 1) < head

    def split(part, low):
        zero = jnp.zeros_like(part)
        return jnp.concatenate([jnp.where(low, part, zero), jnp.where(low, zero, part)], axis=0)

    heads = []
    for at in range(0, width, pair):
        here = slice(at, at + pair)
        scores = lax.dot_general(
            split(query[:, here], low_q), key[:, here], (((1,), (1,)), ((), ())),
            preferred_element_type=F32,
        )
        if same is not None:
            scores = jnp.where(same, scores, -jnp.inf)
        top = jnp.max(scores, axis=-1, keepdims=True)
        raised = jnp.exp2((scores - top) * scale).astype(BF16)
        side = jnp.concatenate([raised[:block], raised[block:]], axis=1)
        total = dot(side, jnp.concatenate([split(value[:, here], low_v), ones], axis=1))
        heads.append((total[:, :pair] / total[:, pair:]).astype(BF16))
    return jnp.concatenate(heads, axis=1)


def same_modulo(queries, keys, stride, start=0):
    query_at = start + lax.broadcasted_iota(jnp.int32, (2 * queries, keys), 0)
    key_at = lax.broadcasted_iota(jnp.int32, (2 * queries, keys), 1)
    return lax.rem(query_at, stride) == lax.rem(key_at, stride)


def attend_and_project(packed, w_out, x, y_ref, heads_ref, stride):
    rows, width = y_ref.shape
    pair = 2 * (width // HEADS)
    block = min(rows, LANES)
    ones = pair_ones(rows, pair // 2)
    keys, values = packed[:, width : 2 * width], packed[:, 2 * width :]
    if rows == block:
        same = same_modulo(block, rows, stride) if stride else None
        heads = attend_heads(packed[:, :width], keys, values, ones, same)
        y_ref[...] = (x + dot(heads, w_out[...])).astype(BF16)
    else:

        @pl.loop(0, rows // block)
        def _(index):
            start = pl.multiple_of(index * block, block)
            here = pl.ds(start, block)
            same = same_modulo(block, rows, stride, start) if stride else None
            heads_ref[here, :] = attend_heads(packed[here, :width], keys, values, ones, same)

        y_ref[...] = (x + dot(heads_ref[...], w_out[...])).astype(BF16)


def spatial_kernel(
    x_hbm, qkv_hbm, out_hbm, next_qkv_hbm, next_out_hbm,
    y_ref, next_qkv_ref, next_out_ref,
    x_ref, qkv_ref, out_ref, packed_ref, heads_ref, sems,
):
    width = x_ref.shape[1]

    def fetch(source, target, at):
        copy = pltpu.make_async_copy(source, target, sems.at[at])
        copy.start()
        return copy

    x_copy = fetch(x_hbm, x_ref, 0)
    copies = [
        fetch(qkv_hbm.at[:, : 2 * width], qkv_ref.at[:, : 2 * width], 1),
        fetch(qkv_hbm.at[:, 2 * width :], qkv_ref.at[:, 2 * width :], 2),
    ]
    out_copy = fetch(out_hbm, out_ref, 4)
    next_copies = [
        fetch(next_qkv_hbm, next_qkv_ref, 5), fetch(next_out_hbm, next_out_ref, 6)
    ]
    x_copy.wait()
    x = x_ref[...].astype(F32)
    normed = norm_rows(x)
    copies[0].wait()
    first = dot(normed, qkv_ref[:, : 2 * width]).astype(BF16)
    copies[1].wait()
    out_copy.wait()
    packed = jnp.concatenate([first, dot(normed, qkv_ref[:, 2 * width :]).astype(BF16)], axis=1)
    if x.shape[0] > LANES:
        packed_ref[...] = packed
        packed = packed_ref
    attend_and_project(packed, out_ref, x, y_ref, heads_ref, 0)
    for copy in next_copies:
        copy.wait()


def spatial_layer(rows, w_qkv, w_out, next_qkv, next_out):
    count, width = rows.shape
    return pl.pallas_call(
        spatial_kernel,
        out_shape=[
            jax.ShapeDtypeStruct((count, width), BF16),
            jax.ShapeDtypeStruct(next_qkv.shape, BF16),
            jax.ShapeDtypeStruct(next_out.shape, BF16),
        ],
        in_specs=[pl.BlockSpec(memory_space=pltpu.HBM)] * 5,
        out_specs=vmem(3),
        scratch_shapes=[
            pltpu.VMEM(rows.shape, BF16),
            pltpu.VMEM(w_qkv.shape, BF16),
            pltpu.VMEM(w_out.shape, BF16),
            pltpu.VMEM((count, 3 * width), BF16),
            pltpu.VMEM((count, width), BF16),
            pltpu.SemaphoreType.DMA((7,)),
        ],
        compiler_params=params(count),
    )(*in_hbm(rows, w_qkv, w_out, next_qkv, next_out))


def temporal_kernel(stride, x_ref, qkv_ref, out_ref, y_ref, packed_ref, heads_ref):
    x = x_ref[...].astype(F32)
    packed = dot(norm_rows(x), qkv_ref[...]).astype(BF16)
    if x.shape[0] > LANES:
        packed_ref[...] = packed
        packed = packed_ref
    attend_and_project(packed, out_ref, x, y_ref, heads_ref, stride)


def temporal_layer(rows, w_qkv, w_out, stride):
    count, width = rows.shape
    return pl.pallas_call(
        functools.partial(temporal_kernel, stride),
        out_shape=jax.ShapeDtypeStruct((count, width), BF16),
        in_specs=vmem(3),
        out_specs=vmem(1)[0],
        scratch_shapes=[
            pltpu.VMEM((count, 3 * width), BF16),
            pltpu.VMEM((count, width), BF16),
        ],
        compiler_params=params(count),
    )(rows, w_qkv, w_out)


def mlp_block(x, up_ref, down_ref):
    normed = norm_rows(x.astype(F32))
    u = dot(normed, up_ref[...])
    half = 0.5 * u
    bend = jnp.tanh(u * (0.7978845608028654 + 0.035677408136300125 * (u * u)))
    hidden = (half + half * bend).astype(BF16)
    return (x.astype(F32) + dot(hidden, down_ref[...])).astype(BF16)


def mlp_kernel(x_ref, up_ref, down_ref, y_ref):
    rows = x_ref.shape[0]
    block = min(rows, LANES)

    @pl.loop(0, rows // block)
    def _(index):
        here = pl.ds(pl.multiple_of(index * block, block), block)
        y_ref[here, :] = mlp_block(x_ref[here, :], up_ref, down_ref)


def mlp_layer(rows, w_up, w_down):
    return pl.pallas_call(
        mlp_kernel,
        out_shape=jax.ShapeDtypeStruct(rows.shape, BF16),
        in_specs=vmem(3),
        out_specs=vmem(1)[0],
        compiler_params=params(rows.shape[0]),
    )(rows, w_up, w_down)


def exchange_order(devices):
    order = np.random.RandomState(24).permutation(devices).tolist()
    first = order.index(min(devices // 2 + 3, devices - 1))
    order[0], order[first] = order[first], order[0]
    return order


def local(clip_tokens, spatial_qkv, spatial_out, temporal_qkv, temporal_out, mlp_up, mlp_down):
    frame_count, patches, width = clip_tokens.shape
    devices = lax.axis_size("seq")
    share = patches // devices
    frames = frame_count * devices
    order = exchange_order(devices)
    mixed = []
    for index in range(frame_count):
        rows, next_qkv, next_out = spatial_layer(
            clip_tokens[index], spatial_qkv, spatial_out, temporal_qkv, temporal_out
        )
        mixed.append(rows)
    mixed = jnp.stack(mixed)
    mixed, mlp_up, mlp_down = lax.optimization_barrier((mixed, mlp_up, mlp_down))
    blocks = mixed.reshape(frame_count, devices, share, width)
    arrived = lax.all_to_all(
        blocks, "seq", split_axis=1, concat_axis=0, axis_index_groups=[order], tiled=True
    )
    tokens = arrived.reshape(frames * share, width)
    after_time = temporal_layer(tokens, next_qkv, next_out, share)
    returned = after_time.reshape(frames, 1, share, width)
    back = lax.all_to_all(
        returned, "seq", split_axis=0, concat_axis=1, axis_index_groups=[order], tiled=True
    )
    result = mlp_layer(back.reshape(frame_count * patches, width), mlp_up, mlp_down)
    return result.reshape(frame_count, patches, width)


def solution(mesh):
    in_specs = (P(("groups", "seq"), None, None), P(), P(), P(), P(), P(), P())
    out_specs = P(("groups", "seq"), None, None)
    return jax.shard_map(local, mesh=mesh, in_specs=in_specs, out_specs=out_specs, check_vma=False)
```

```python
import functools

import jax
import jax.numpy as jnp
import numpy as np
from jax import lax
from jax.experimental import pallas as pl
from jax.experimental.pallas import tpu as pltpu
from jax.sharding import PartitionSpec as P

HEADS = 8
LANES = 128
BF16 = jnp.bfloat16
F32 = jnp.float32
MIB = 1024 * 1024


def vmem_limit(rows):
    return 10 * MIB + rows * 32 * 1024


def params(rows):
    return pltpu.CompilerParams(vmem_limit_bytes=vmem_limit(rows))


def in_hbm(*arrays):
    return tuple(pltpu.with_memory_space_constraint(each, pltpu.HBM) for each in arrays)


def vmem(count):
    return [pl.BlockSpec(memory_space=pltpu.VMEM)] * count


def norm_rows(values):
    center = values - jnp.mean(values, axis=-1, keepdims=True)
    spread = jnp.mean(center * center, axis=-1, keepdims=True)
    return (center * lax.rsqrt(spread + 1e-05)).astype(BF16)


def dot(left, right):
    return jnp.dot(left, right, preferred_element_type=F32)


def norm_dot(x, weights):
    rows = x.shape[0]
    stacked = jnp.concatenate([x, jnp.ones((16, x.shape[1]), BF16)], axis=0)
    product = dot(stacked, weights)
    values = x.astype(F32)
    mean = jnp.mean(values, axis=-1, keepdims=True)
    center = values - mean
    spread = jnp.mean(center * center, axis=-1, keepdims=True)
    return (product[:rows] - mean * product[rows : rows + 1]) * lax.rsqrt(spread + 1e-05)


def pair_ones(keys, head):
    low = lax.broadcasted_iota(jnp.int32, (keys, 2 * head), 1) < head
    return jnp.concatenate(
        [jnp.where(low, 1.0, 0.0), jnp.where(low, 0.0, 1.0)], axis=0
    ).astype(BF16)


def attend_heads(query, key, value, ones, same):
    block, width = query.shape
    head = width // HEADS
    pair = 2 * head
    scale = head ** (-0.5) * 1.4426950408889634
    low_q = lax.broadcasted_iota(jnp.int32, (block, pair), 1) < head
    low_v = lax.broadcasted_iota(jnp.int32, (value.shape[0], pair), 1) < head

    def split(part, low):
        zero = jnp.zeros_like(part)
        return jnp.concatenate([jnp.where(low, part, zero), jnp.where(low, zero, part)], axis=0)

    heads = []
    for at in range(0, width, pair):
        here = slice(at, at + pair)
        scores = lax.dot_general(
            split(query[:, here], low_q), key[:, here], (((1,), (1,)), ((), ())),
            preferred_element_type=F32,
        )
        if same is not None:
            scores = jnp.where(same, scores, -jnp.inf)
        top = jnp.max(scores, axis=-1, keepdims=True)
        raised = jnp.exp2((scores - top) * scale).astype(BF16)
        side = jnp.concatenate([raised[:block], raised[block:]], axis=1)
        total = dot(side, jnp.concatenate([split(value[:, here], low_v), ones], axis=1))
        heads.append((total[:, :pair] / total[:, pair:]).astype(BF16))
    return jnp.concatenate(heads, axis=1)


def same_modulo(queries, keys, stride, start=0):
    query_at = start + lax.broadcasted_iota(jnp.int32, (2 * queries, keys), 0)
    key_at = lax.broadcasted_iota(jnp.int32, (2 * queries, keys), 1)
    return lax.rem(query_at, stride) == lax.rem(key_at, stride)


def attend_and_project(packed, w_out, x, y_ref, heads_ref, stride):
    rows, width = y_ref.shape
    pair = 2 * (width // HEADS)
    block = min(rows, LANES)
    ones = pair_ones(rows, pair // 2)
    keys, values = packed[:, width : 2 * width], packed[:, 2 * width :]
    if rows == block:
        same = same_modulo(block, rows, stride) if stride else None
        heads = attend_heads(packed[:, :width], keys, values, ones, same)
        y_ref[...] = (x + dot(heads, w_out[...])).astype(BF16)
    else:

        @pl.loop(0, rows // block)
        def _(index):
            start = pl.multiple_of(index * block, block)
            here = pl.ds(start, block)
            same = same_modulo(block, rows, stride, start) if stride else None
            heads_ref[here, :] = attend_heads(packed[here, :width], keys, values, ones, same)

        y_ref[...] = (x + dot(heads_ref[...], w_out[...])).astype(BF16)


def spatial_kernel(
    x_hbm, qkv_hbm, out_hbm, next_qkv_hbm, next_out_hbm,
    y_ref, next_qkv_ref, next_out_ref,
    x_ref, qkv_ref, out_ref, packed_ref, heads_ref, sems,
):
    width = x_ref.shape[1]

    def fetch(source, target, at):
        copy = pltpu.make_async_copy(source, target, sems.at[at])
        copy.start()
        return copy

    x_copy = fetch(x_hbm, x_ref, 0)
    copies = [
        fetch(qkv_hbm.at[:, : 2 * width], qkv_ref.at[:, : 2 * width], 1),
        fetch(qkv_hbm.at[:, 2 * width :], qkv_ref.at[:, 2 * width :], 2),
    ]
    out_copy = fetch(out_hbm, out_ref, 4)
    next_copies = [
        fetch(next_qkv_hbm, next_qkv_ref, 5), fetch(next_out_hbm, next_out_ref, 6)
    ]
    x_copy.wait()
    x = x_ref[...].astype(F32)
    normed = norm_rows(x)
    copies[0].wait()
    first = dot(normed, qkv_ref[:, : 2 * width]).astype(BF16)
    copies[1].wait()
    out_copy.wait()
    packed = jnp.concatenate([first, dot(normed, qkv_ref[:, 2 * width :]).astype(BF16)], axis=1)
    if x.shape[0] > LANES:
        packed_ref[...] = packed
        packed = packed_ref
    attend_and_project(packed, out_ref, x, y_ref, heads_ref, 0)
    for copy in next_copies:
        copy.wait()


def spatial_layer(rows, w_qkv, w_out, next_qkv, next_out):
    count, width = rows.shape
    return pl.pallas_call(
        spatial_kernel,
        out_shape=[
            jax.ShapeDtypeStruct((count, width), BF16),
            jax.ShapeDtypeStruct(next_qkv.shape, BF16),
            jax.ShapeDtypeStruct(next_out.shape, BF16),
        ],
        in_specs=[pl.BlockSpec(memory_space=pltpu.HBM)] * 5,
        out_specs=vmem(3),
        scratch_shapes=[
            pltpu.VMEM(rows.shape, BF16),
            pltpu.VMEM(w_qkv.shape, BF16),
            pltpu.VMEM(w_out.shape, BF16),
            pltpu.VMEM((count, 3 * width), BF16),
            pltpu.VMEM((count, width), BF16),
            pltpu.SemaphoreType.DMA((7,)),
        ],
        compiler_params=params(count),
    )(*in_hbm(rows, w_qkv, w_out, next_qkv, next_out))


def temporal_kernel(stride, x_ref, qkv_ref, out_ref, y_ref, packed_ref, heads_ref):
    x = x_ref[...].astype(F32)
    packed = norm_dot(x_ref[...], qkv_ref[...]).astype(BF16)
    if x.shape[0] > LANES:
        packed_ref[...] = packed
        packed = packed_ref
    attend_and_project(packed, out_ref, x, y_ref, heads_ref, stride)


def temporal_layer(rows, w_qkv, w_out, stride):
    count, width = rows.shape
    return pl.pallas_call(
        functools.partial(temporal_kernel, stride),
        out_shape=jax.ShapeDtypeStruct((count, width), BF16),
        in_specs=vmem(3),
        out_specs=vmem(1)[0],
        scratch_shapes=[
            pltpu.VMEM((count, 3 * width), BF16),
            pltpu.VMEM((count, width), BF16),
        ],
        compiler_params=params(count),
    )(rows, w_qkv, w_out)


def mlp_block(x, up_ref, down_ref):
    u = norm_dot(x, up_ref[...])
    half = 0.5 * u
    bend = jnp.tanh(u * (0.7978845608028654 + 0.035677408136300125 * (u * u)))
    hidden = (half + half * bend).astype(BF16)
    return (x.astype(F32) + dot(hidden, down_ref[...])).astype(BF16)


def mlp_kernel(x_ref, up_ref, down_ref, y_ref):
    rows = x_ref.shape[0]
    block = min(rows, LANES)

    @pl.loop(0, rows // block)
    def _(index):
        here = pl.ds(pl.multiple_of(index * block, block), block)
        y_ref[here, :] = mlp_block(x_ref[here, :], up_ref, down_ref)


def mlp_layer(rows, w_up, w_down):
    return pl.pallas_call(
        mlp_kernel,
        out_shape=jax.ShapeDtypeStruct(rows.shape, BF16),
        in_specs=vmem(3),
        out_specs=vmem(1)[0],
        compiler_params=params(rows.shape[0]),
    )(rows, w_up, w_down)


def exchange_order(devices):
    order = np.random.RandomState(24).permutation(devices).tolist()
    first = order.index(min(devices // 2 + 3, devices - 1))
    order[0], order[first] = order[first], order[0]
    return order


def local(clip_tokens, spatial_qkv, spatial_out, temporal_qkv, temporal_out, mlp_up, mlp_down):
    frame_count, patches, width = clip_tokens.shape
    devices = lax.axis_size("seq")
    share = patches // devices
    frames = frame_count * devices
    order = exchange_order(devices)
    mixed = []
    for index in range(frame_count):
        rows, next_qkv, next_out = spatial_layer(
            clip_tokens[index], spatial_qkv, spatial_out, temporal_qkv, temporal_out
        )
        mixed.append(rows)
    mixed = jnp.stack(mixed)
    mixed, mlp_up, mlp_down = lax.optimization_barrier((mixed, mlp_up, mlp_down))
    blocks = mixed.reshape(frame_count, devices, share, width)
    arrived = lax.all_to_all(
        blocks, "seq", split_axis=1, concat_axis=0, axis_index_groups=[order], tiled=True
    )
    tokens = arrived.reshape(frames * share, width)
    after_time = temporal_layer(tokens, next_qkv, next_out, share)
    returned = after_time.reshape(frames, 1, share, width)
    back = lax.all_to_all(
        returned, "seq", split_axis=0, concat_axis=1, axis_index_groups=[order], tiled=True
    )
    result = mlp_layer(back.reshape(frame_count * patches, width), mlp_up, mlp_down)
    return result.reshape(frame_count, patches, width)


def solution(mesh):
    in_specs = (P(("groups", "seq"), None, None), P(), P(), P(), P(), P(), P())
    out_specs = P(("groups", "seq"), None, None)
    return jax.shard_map(local, mesh=mesh, in_specs=in_specs, out_specs=out_specs, check_vma=False)
```
